512 devices in a mesh: param: 32 (over x, y), ex: 16 (over z, core).
Axes of the slice: x: 4, y: 8, z: 8, core: 2. Of those that a mesh axis runs over, the one named last changes fastest.
Arguments:
- act_factor: bfloat16 [16384, 4096], P('ex', 'param'), may hold values from -6 to 6
- grad_factor: bfloat16 [16384, 4096], P('ex', 'param'), may hold values from -6 to 6
- proj_bank: bfloat16 [16, 128, 128], replicated, may hold values from -0.5 to 0.5
- tile_rows: int32 [256], replicated, may hold values from 0 to 31
- tile_cols: int32 [256], replicated, may hold values from 0 to 31
- tile_out: int32 [256], replicated, may hold values from 0 to 7
- bank_left: int32 [256], replicated, may hold values from 0 to 15
- bank_right: int32 [256], replicated, may hold values from 0 to 15
- owner_map: int32 [16, 32], P('ex'), may hold values from 0 to 31, each once within a row
Outputs:
- features: float32 [512, 1024], P(('ex', 'param'))
- factor_r: float32 [1024, 1024], P('param', 'ex')
The draws below stay inside these ranges and needn't reach their ends.
Inputs may be any that keep to these rules, and one draw needn't show every extreme that they name: Each row of owner_map is a permutation of the 32 examples of its group.
All inputs are finite; a program needn't handle non-finite values.
Results may differ from the reference program's by a relative error of at most 0.0003.
Values may be sent and summed in bfloat16 or wider, within the bound.
No kernel may reach another device: no remote copies, remote signals or barrier semaphores. Data moves between devices by JAX's collectives and lax.ppermute only.
A program may use at most 64 MiB of HBM per device.

```python
import math
import jax
import jax.numpy as jnp
from jax import lax

D = 4096
K = 1024
TILE = 128
SLOTS = 256
BANK = 16
SEQ = 32
EX_GRP = 32
EXAMPLES = 512
TOKENS = 16384
NBLK = 32
NOUT = 8
N_EX = 16


def set_ends(result, rng, smallest, high):
    longest = result.shape.index(max(result.shape))
    spots = []
    for shift in (0, 1):
        where = [jax.random.randint(jax.random.fold_in(rng, axis), (), 0, length) for axis, length in enumerate(result.shape)]
        where[longest] = (where[longest] + shift) % result.shape[longest]
        spots.append(tuple(where))
    return result.at[spots[0]].set(smallest).at[spots[1]].set(high)


def levels(rng, extent, pieces, smallest, high):
    level, own = 1.0, jax.random.fold_in(rng, 6)
    for axis_at, shards_of in pieces:
        heights = jnp.exp(jax.random.uniform(jax.random.fold_in(own, axis_at), (shards_of,), jnp.float32, smallest / len(pieces), high / len(pieces)))
        level = level * jnp.repeat(heights, extent[axis_at] // shards_of).reshape([-1 if axis == axis_at else 1 for axis in range(len(extent))])
    return level


def centred(rng, dims, width, most, cuts=(), held_as=jnp.bfloat16):
    result = width * jax.random.normal(rng, dims, jnp.float32)
    if cuts:
        result = result * levels(rng, dims, cuts, -0.22, 0.18)
    return jnp.clip(result, -most, most).astype(held_as)


def setup_inputs(seed: int = 0) -> dict:
    keys = jax.random.split(jax.random.key(seed), 10)
    act_factor = centred(keys[0], (TOKENS, D), 1.0, 6.0, ((0, 16), (1, 32)))
    grad_factor = centred(keys[1], (TOKENS, D), 1.0, 6.0, ((0, 16), (1, 32)))
    proj_bank = centred(keys[2], (BANK, TILE, TILE), TILE ** -0.5, 0.5)
    tile_rows = set_ends(jax.random.randint(keys[3], (SLOTS,), 0, NBLK), jax.random.fold_in(keys[3], 1), 0, NBLK - 1).astype(jnp.int32)
    tile_cols = set_ends(jax.random.randint(keys[4], (SLOTS,), 0, NBLK), jax.random.fold_in(keys[4], 1), 0, NBLK - 1).astype(jnp.int32)
    tile_out = set_ends(jax.random.randint(keys[5], (SLOTS,), 0, NOUT), jax.random.fold_in(keys[5], 1), 0, NOUT - 1).astype(jnp.int32)
    bank_left = set_ends(jax.random.randint(keys[6], (SLOTS,), 0, BANK), jax.random.fold_in(keys[6], 1), 0, BANK - 1).astype(jnp.int32)
    bank_right = set_ends(jax.random.randint(keys[7], (SLOTS,), 0, BANK), jax.random.fold_in(keys[7], 1), 0, BANK - 1).astype(jnp.int32)
    owner_map = jax.vmap(lambda own: jax.random.permutation(own, EX_GRP))(jax.random.split(keys[8], N_EX)).reshape((N_EX, EX_GRP)).astype(jnp.int32)
    return dict(act_factor=act_factor, grad_factor=grad_factor, proj_bank=proj_bank, tile_rows=tile_rows, tile_cols=tile_cols, tile_out=tile_out, bank_left=bank_left, bank_right=bank_right, owner_map=owner_map)


damping = 0.25

def project_rows(act_rows, grad_rows, proj_bank, tile_rows, tile_cols, tile_out, bank_left, bank_right):
    ex_count = act_rows.shape[0]
    token_count = ex_count * SEQ
    out_tiles = K // TILE
    slot_count = tile_rows.shape[0]
    group_size = math.gcd(slot_count, 32)
    act_blocks = act_rows.reshape(token_count, D // TILE, TILE)
    grad_blocks = grad_rows.reshape(token_count, D // TILE, TILE)
    picked_ids = tuple((id_list.reshape(slot_count // group_size, group_size) for id_list in (tile_rows, tile_cols, tile_out, bank_left, bank_right)))
    tile_index = jnp.arange(out_tiles, dtype=jnp.int32)

    def add_group(summed, picked):
        row_ids, col_ids, out_ids, left_ids, right_ids = picked
        left_proj = jnp.einsum('tsi,sik->stk', jnp.take(act_blocks, row_ids, axis=1).astype(jnp.float32), jnp.take(proj_bank, left_ids, axis=0).astype(jnp.float32))
        right_proj = jnp.einsum('tsi,sik->stk', jnp.take(grad_blocks, col_ids, axis=1).astype(jnp.float32), jnp.take(proj_bank, right_ids, axis=0).astype(jnp.float32))
        per_example = (left_proj * right_proj).reshape(group_size, ex_count, SEQ, TILE).sum(axis=2)
        matches = (out_ids[:, None] == tile_index[None, :]).astype(jnp.float32)
        return (summed + lax.optimization_barrier(jnp.sum(matches[:, None, :, None] * per_example[:, :, None, :], axis=0)), None)
    summed, unused = lax.scan(add_group, jnp.zeros((ex_count, out_tiles, TILE), jnp.float32), picked_ids)
    return summed.reshape(ex_count, K) * (1.0 / math.sqrt(SEQ * slot_count / out_tiles))

def reference(act_factor, grad_factor, proj_bank, tile_rows, tile_cols, tile_out, bank_left, bank_right, owner_map):
    act_groups = act_factor.reshape(N_EX, EX_GRP, SEQ, D)
    grad_groups = grad_factor.reshape(N_EX, EX_GRP, SEQ, D)

    def one_group(operands):
        act_group, grad_group, ordering = operands
        return project_rows(jnp.take(act_group, ordering, axis=0), jnp.take(grad_group, ordering, axis=0), proj_bank, tile_rows, tile_cols, tile_out, bank_left, bank_right)
    features = lax.map(one_group, (act_groups, grad_groups, owner_map)).reshape(EXAMPLES, K)
    gram_matrix = jnp.dot(features.T, features, precision=lax.Precision.HIGHEST) / EXAMPLES + damping * jnp.eye(K, dtype=jnp.float32)
    factor_r = jnp.linalg.cholesky(gram_matrix).T
    return (features, factor_r)
```

```python
import functools
import math

import jax
import jax.numpy as jnp
from jax import lax
from jax.experimental import pallas as pl
from jax.experimental.pallas import tpu as pltpu
from jax.sharding import PartitionSpec as P

TILE = 128
SUB = 8
DAMPING = 0.25
PIECES = 3
AHEAD = 6
f32, bf16 = jnp.float32, jnp.bfloat16


def project_kernel(
    seq_len, scale, rows_ref, cols_ref, outs_ref, lefts_ref, rights_ref, x_ref, bank_ref, feat_ref, table, acc
):
    banks = bank_ref.shape[0]
    for pair in range(banks // 2):
        tiles = jnp.concatenate([bank_ref[2 * pair], bank_ref[2 * pair + 1]], axis=1)
        both = jnp.dot(x_ref[...], tiles, preferred_element_type=f32)
        table[2 * pair] = both[:, :TILE]
        table[2 * pair + 1] = both[:, TILE:]
    acc[...] = jnp.zeros_like(acc)
    unroll = 8

    def add_slots(group, carry):
        for k in range(unroll):
            s = group * unroll + k
            left_at = pl.multiple_of(rows_ref[s] * (2 * seq_len), seq_len)
            right_at = pl.multiple_of(cols_ref[s] * (2 * seq_len) + seq_len, seq_len)
            left = table[lefts_ref[s], pl.ds(left_at, seq_len), :]
            right = table[rights_ref[s], pl.ds(right_at, seq_len), :]
            term = jnp.sum((left * right).reshape(seq_len // SUB, SUB, TILE), axis=0)
            acc[outs_ref[s]] += term
        return carry

    lax.fori_loop(0, rows_ref.shape[0] // unroll, add_slots, 0)
    feat_ref[...] = jnp.sum(acc[...], axis=1) * scale


def project(x, bank, ids, seq_len, out_tiles):
    scale = 1.0 / math.sqrt(seq_len * ids[0].shape[0] / out_tiles)
    smem = pl.BlockSpec(memory_space=pltpu.SMEM)
    vmem = pl.BlockSpec(memory_space=pltpu.VMEM)
    return pl.pallas_call(
        functools.partial(project_kernel, seq_len, scale),
        out_shape=jax.ShapeDtypeStruct((out_tiles, TILE), f32),
        in_specs=[smem] * 5 + [vmem] * 2,
        out_specs=vmem,
        scratch_shapes=[
            pltpu.VMEM((bank.shape[0], x.shape[0], TILE), f32),
            pltpu.VMEM((out_tiles, SUB, TILE), f32),
        ],
        compiler_params=pltpu.CompilerParams(vmem_limit_bytes=40 * 2**20),
        name="project",
    )(*ids, x, bank)


def factor_block(rows):
    groups = len(rows)
    lane = lax.broadcasted_iota(jnp.int32, (SUB, TILE), 1)
    sub = lax.broadcasted_iota(jnp.int32, (SUB, TILE), 0)
    rows = list(rows)

    def spread(column, first):
        return {q: jnp.broadcast_to(rows[q][:, column : column + 1], (SUB, TILE)) for q in range(first, groups)}

    columns = {c: spread(c, 0) for c in range(AHEAD)}
    for i in range(TILE):
        q, s = divmod(i, SUB)
        columns = {c: {p: v for p, v in held.items() if p >= q} for c, held in columns.items()}
        pivot = columns.pop(i)
        inverse = 1.0 / jnp.broadcast_to(pivot[q][s : s + 1, :], (SUB, TILE))
        at_pivot, below = lane == i, sub > s
        row = jnp.broadcast_to(rows[q][s : s + 1, :], (SUB, TILE))
        weights = jnp.where(at_pivot, 1.0, row) * inverse
        own = jnp.where(below, pivot[q], 0.0)
        for c in sorted(columns):
            weight = jnp.broadcast_to(columns[c][q][s : s + 1, :], (SUB, TILE)) * inverse
            for p in columns[c]:
                columns[c][p] = columns[c][p] - (own if p == q else pivot[p]) * weight
        if s < SUB - 1:
            rows[q] = jnp.where(at_pivot & below, 0.0, rows[q]) - own * weights
        for p in range(q + 1, groups):
            rows[p] = jnp.where(at_pivot, 0.0, rows[p]) - pivot[p] * weights
        if i + AHEAD < TILE:
            columns[i + AHEAD] = spread(i + AHEAD, (i + 1) // SUB)
    upper, inverse_lower = [], []
    for q in range(groups):
        r = sub + SUB * q
        diagonal = jnp.sum(jnp.where(lane == r, rows[q], 0.0), axis=1, keepdims=True)
        root = lax.rsqrt(diagonal)
        upper.append(jnp.where(lane >= r, rows[q], 0.0) * root)
        inverse_lower.append(jnp.where(lane < r, rows[q], jnp.where(lane == r, 1.0, 0.0)) * root)
    return jnp.concatenate(upper, 0), jnp.concatenate(inverse_lower, 0)


def split(x):
    pieces = []
    for k in range(PIECES):
        piece = x.astype(bf16)
        pieces.append(piece)
        if k < PIECES - 1:
            x = x - piece.astype(f32)
    return pieces


def times_t(a, b):
    total = None
    for i, k in sorted(((i, k) for i in range(PIECES) for k in range(PIECES) if i + k < max(PIECES, 3)), key=lambda ik: -sum(ik)):
        term = lax.dot_general(a[i], b[k], (((1,), (1,)), ((), ())), preferred_element_type=f32)
        total = term if total is None else total + term
    return total


def factor_kernel(place_ref, own_ref, other_ref, out_ref, lower, panels, *pieces):
    ft, lp = pieces[:PIECES], pieces[PIECES:]
    half, nb, _ = own_ref.shape
    scale = 1.0 / (2 * half)
    for h, ref in enumerate((own_ref, other_ref)):
        for b in range(nb):
            for k, piece in enumerate(split(ref[:, b, :].T)):
                ft[k][b * TILE : (b + 1) * TILE, h * half : (h + 1) * half] = piece

    def feats(lo, hi):
        return [ref[lo * TILE : hi * TILE, :] for ref in ft]

    def lows(lo, hi, to):
        return [ref[lo * TILE : hi * TILE, : to * TILE] for ref in lp]

    def put(lo, hi, c, value):
        lower[lo * TILE : hi * TILE, c * TILE : (c + 1) * TILE] = value
        for ref, piece in zip(lp, split(value)):
            ref[lo * TILE : hi * TILE, c * TILE : (c + 1) * TILE] = piece

    shape = (TILE, TILE)
    eye = lax.broadcasted_iota(jnp.int32, shape, 0) == lax.broadcasted_iota(jnp.int32, shape, 1)

    def diagonal(j, known):
        block = times_t(feats(j, j + 1), feats(j, j + 1)) * scale + jnp.where(eye, DAMPING, 0.0)
        if known:
            block = block - times_t(lows(j, j + 1, known), lows(j, j + 1, known))
        return block

    for i in range(nb):
        for c in range(i + 1, nb):
            lower[i * TILE : (i + 1) * TILE, c * TILE : (c + 1) * TILE] = jnp.zeros(shape, f32)

    block, inverse = diagonal(0, 0), None
    for j in range(nb):
        if j >= 1 and j + 1 < nb:
            put(j + 1, nb, j - 1, times_t(split(panels[(j - 1) % 2, (j + 1) * TILE :, :]), inverse))
        if j + 1 < nb:
            panel = times_t(feats(j + 1, nb), feats(j, j + 1)) * scale
            if j:
                panel = panel - times_t(lows(j + 1, nb, j), lows(j, j + 1, j))
            panels[j % 2, (j + 1) * TILE :, :] = panel
            ahead = diagonal(j + 1, j)
        upper, inverse = factor_block([block[SUB * q : SUB * (q + 1), :] for q in range(TILE // SUB)])
        lower[j * TILE : (j + 1) * TILE, j * TILE : (j + 1) * TILE] = upper.T
        if j + 1 < nb:
            inverse = split(inverse)
            first = times_t(split(panels[j % 2, (j + 1) * TILE : (j + 2) * TILE, :]), inverse)
            put(j + 1, j + 2, j, first)
            first = split(first)
            block = ahead - times_t(first, first)

    height, width = out_ref.shape
    ex, param = place_ref[0], place_ref[1]
    per_tile = TILE // height
    taken = lower[pl.ds(pl.multiple_of(ex * width, width), width), pl.ds(pl.multiple_of(param // per_tile * TILE, TILE), TILE)]
    flipped = taken.T
    result = flipped[:height]
    for k in range(1, per_tile):
        result = jnp.where(param % per_tile == k, flipped[k * height : (k + 1) * height], result)
    out_ref[...] = result


def factor(place, own, other, block_shape):
    half, nb, _ = own.shape
    width = nb * TILE
    vmem = pl.BlockSpec(memory_space=pltpu.VMEM)
    return pl.pallas_call(
        factor_kernel,
        out_shape=jax.ShapeDtypeStruct(block_shape, f32),
        in_specs=[pl.BlockSpec(memory_space=pltpu.SMEM), vmem, vmem],
        out_specs=vmem,
        scratch_shapes=[pltpu.VMEM((width, width), f32), pltpu.VMEM((2, width, TILE), f32)]
        + [pltpu.VMEM((width, 2 * half), bf16)] * PIECES
        + [pltpu.VMEM((width, width), bf16)] * PIECES,
        compiler_params=pltpu.CompilerParams(vmem_limit_bytes=48 * 2**20),
        name="factor",
    )(place, own, other)


def per_device(
    ex_size, act_factor, grad_factor, proj_bank, tile_rows, tile_cols, tile_out, bank_left, bank_right, owner_map
):
    group = owner_map.shape[1]
    tokens, width = act_factor.shape
    seq_len = tokens // group
    out_tiles = 1024 // width
    ex, param = lax.axis_index("ex"), lax.axis_index("param")

    both = jnp.concatenate([f.reshape(group, seq_len, width) for f in (act_factor, grad_factor)], axis=1)
    both = lax.all_to_all(both, "param", split_axis=0, concat_axis=0, tiled=True)
    feats = project(
        both.reshape(2 * tokens, width),
        proj_bank,
        (tile_rows, tile_cols, tile_out, bank_left, bank_right),
        seq_len,
        out_tiles,
    )

    chips = ex_size // 2 * group
    cores = [[(2 * z + core) * group + p for z in range(ex_size // 2) for p in range(group)] for core in range(2)]
    own = lax.all_to_all(
        jnp.broadcast_to(feats[None], (chips,) + feats.shape),
        ("ex", "param"),
        split_axis=0,
        concat_axis=0,
        axis_index_groups=cores,
        tiled=True,
    )
    other = lax.ppermute(own, "ex", [(i, i ^ 1) for i in range(ex_size)])

    mine = ex // 2 * group + owner_map[0, param]
    features = lax.dynamic_slice(own, (mine, 0, 0), (1, out_tiles, width)).reshape(1, out_tiles * width)
    block = (out_tiles * width // group, out_tiles * width // ex_size)
    r_block = factor(jnp.stack([ex, param]).astype(jnp.int32), own, other, block)
    return features, r_block


def solution(mesh):
    placed = (P("ex", "param"), P("ex", "param"), P(), P(), P(), P(), P(), P(), P("ex", None))
    return jax.shard_map(
        functools.partial(per_device, mesh.shape["ex"]),
        mesh=mesh,
        in_specs=placed,
        out_specs=(P(("ex", "param"), None), P("param", "ex")),
        check_vma=False,
    )
```

```python
import functools
import math

import jax
import jax.numpy as jnp
from jax import lax
from jax.experimental import pallas as pl
from jax.experimental.pallas import tpu as pltpu
from jax.sharding import PartitionSpec as P

TILE = 128
SUB = 8
DAMPING = 0.25
PIECES = 3
AHEAD = 4
LEVELS = 32767.0
STEPS = 16.0
f32, bf16 = jnp.float32, jnp.bfloat16


def project_kernel(
    seq_len, scale, rows_ref, cols_ref, outs_ref, lefts_ref, rights_ref, x_ref, bank_ref, feat_ref, table, acc
):
    banks = bank_ref.shape[0]
    for pair in range(banks // 2):
        tiles = jnp.concatenate([bank_ref[2 * pair], bank_ref[2 * pair + 1]], axis=1)
        both = jnp.dot(x_ref[...], tiles, preferred_element_type=f32)
        table[2 * pair] = both[:, :TILE]
        table[2 * pair + 1] = both[:, TILE:]
    acc[...] = jnp.zeros_like(acc)
    unroll = 8

    def add_slots(group, carry):
        for k in range(unroll):
            s = group * unroll + k
            left_at = pl.multiple_of(rows_ref[s] * (2 * seq_len), seq_len)
            right_at = pl.multiple_of(cols_ref[s] * (2 * seq_len) + seq_len, seq_len)
            left = table[lefts_ref[s], pl.ds(left_at, seq_len), :]
            right = table[rights_ref[s], pl.ds(right_at, seq_len), :]
            term = jnp.sum((left * right).reshape(seq_len // SUB, SUB, TILE), axis=0)
            acc[outs_ref[s]] += term
        return carry

    lax.fori_loop(0, rows_ref.shape[0] // unroll, add_slots, 0)
    feat_ref[...] = jnp.sum(acc[...], axis=1) * scale


def project(x, bank, ids, seq_len, out_tiles):
    scale = 1.0 / math.sqrt(seq_len * ids[0].shape[0] / out_tiles)
    smem = pl.BlockSpec(memory_space=pltpu.SMEM)
    vmem = pl.BlockSpec(memory_space=pltpu.VMEM)
    return pl.pallas_call(
        functools.partial(project_kernel, seq_len, scale),
        out_shape=jax.ShapeDtypeStruct((out_tiles, TILE), f32),
        in_specs=[smem] * 5 + [vmem] * 2,
        out_specs=vmem,
        scratch_shapes=[
            pltpu.VMEM((bank.shape[0], x.shape[0], TILE), f32),
            pltpu.VMEM((out_tiles, SUB, TILE), f32),
        ],
        compiler_params=pltpu.CompilerParams(vmem_limit_bytes=40 * 2**20),
        name="project",
    )(*ids, x, bank)


def factor_block(rows):
    groups = len(rows)
    lane = lax.broadcasted_iota(jnp.int32, (SUB, TILE), 1)
    sub = lax.broadcasted_iota(jnp.int32, (SUB, TILE), 0)
    rows = list(rows)

    def column(p, c):
        return jnp.broadcast_to(rows[p][:, c : c + 1], (SUB, TILE))

    def entry(x, s):
        return jnp.broadcast_to(x[s : s + 1, :], (SUB, TILE))

    def wanted(i, first):
        for c in range(max(i, 0), min(TILE, i + SUB + 1)):
            for p in range(first, groups):
                if c <= i + AHEAD or p <= c // SUB:
                    yield c, p

    spread = {(c, p): column(p, c) for c, p in wanted(-1, 0)}
    small, upper, inverse_lower = {}, [], []
    for i in range(TILE):
        q, s = divmod(i, SUB)
        if s == 0:
            small = {(k, l): entry(spread[SUB * q + l, q], k) for k in range(SUB) for l in range(k, SUB)}
            root = None
        inverse = 1.0 / small[s, s]
        one_root = lax.rsqrt(small[s, s])
        root = one_root if root is None else jnp.where(sub == s, one_root, root)
        weights = {SUB * q + l: small[s, l] * inverse for l in range(s + 1, SUB)}
        for l in range(s + 1, SUB):
            for m in range(l, SUB):
                small[l, m] = small[l, m] - small[s, m] * weights[SUB * q + l]
        at_pivot, below = lane == i, sub > s
        row = jnp.where(at_pivot, 1.0, entry(rows[q], s)) * inverse
        own = jnp.where(below, spread[i, q], 0.0)
        for c in sorted({c for c, _ in spread if c > i}):
            if c not in weights:
                weights[c] = entry(spread[c, q], s) * inverse
            for p in range(q, groups):
                if (c, p) in spread:
                    spread[c, p] = spread[c, p] - (own if p == q else spread[i, p]) * weights[c]
        if s < SUB - 1:
            rows[q] = jnp.where(at_pivot & below, 0.0, rows[q]) - own * row
        for p in range(q + 1, groups):
            rows[p] = jnp.where(at_pivot, 0.0, rows[p]) - spread[i, p] * row
        if s == SUB - 1:
            r = sub + SUB * q
            upper.append(jnp.where(lane >= r, rows[q], 0.0) * root)
            inverse_lower.append(jnp.where(lane < r, rows[q], jnp.where(lane == r, 1.0, 0.0)) * root)
        first = (i + 1) // SUB
        spread = {(c, p): v for (c, p), v in spread.items() if c > i and p >= first}
        for c, p in wanted(i, first):
            if c > i and (c, p) not in spread:
                spread[c, p] = column(p, c)
    return jnp.concatenate(upper, 0), jnp.concatenate(inverse_lower, 0)


def split(x):
    pieces = []
    for k in range(PIECES):
        piece = x.astype(bf16)
        pieces.append(piece)
        if k < PIECES - 1:
            x = x - piece.astype(f32)
    return pieces


def times_t(a, b):
    total = None
    for i, k in sorted(((i, k) for i in range(PIECES) for k in range(PIECES) if i + k < max(PIECES, 3)), key=lambda ik: -sum(ik)):
        term = lax.dot_general(a[i], b[k], (((1,), (1,)), ((), ())), preferred_element_type=f32)
        total = term if total is None else total + term
    return total


def encode(rows):
    count, blocks, width = rows.shape
    top = jnp.max(jnp.abs(rows), axis=(1, 2), keepdims=True)
    step = jnp.ceil(STEPS * jnp.log2(jnp.maximum(top, 1e-30)))
    coded = jnp.clip(jnp.round(rows * (LEVELS * jnp.exp2(step / -STEPS))), -LEVELS, LEVELS)
    scales = jnp.broadcast_to(step[:, 0], (count, width))
    parts = [coded.reshape(count * blocks, width), scales, jnp.zeros((-count % 16, width), f32)]
    return jnp.concatenate(parts, axis=0).astype(jnp.int16)


def factor_kernel(place_ref, own_ref, other_ref, out_ref, lower, panels, feat, *pieces):
    ft, lp = pieces[:PIECES], pieces[PIECES:]
    examples, nb, _ = feat.shape
    peers = own_ref.shape[0]
    count = examples // (2 * peers)
    scale = 1.0 / examples
    for h, ref in enumerate((own_ref, other_ref)):

        def decode(peer, carry):
            coded = ref[peer].astype(jnp.int32).astype(f32)
            steps = coded[count * nb : count * nb + count]
            scales = jnp.exp2(steps * (1.0 / STEPS)) * (1.0 / LEVELS)
            values = coded[: count * nb].reshape(count, nb, TILE) * jnp.broadcast_to(scales[:, None, :], (count, nb, TILE))
            feat[pl.ds(h * peers * count + peer * count, count)] = values
            return carry

        lax.fori_loop(0, peers, decode, 0)
    for b in range(nb):
        for k, piece in enumerate(split(feat[:, b, :].T)):
            ft[k][b * TILE : (b + 1) * TILE, :] = piece

    def feats(lo, hi):
        return [ref[lo * TILE : hi * TILE, :] for ref in ft]

    def lows(lo, hi, to):
        return [ref[lo * TILE : hi * TILE, : to * TILE] for ref in lp]

    def put(lo, hi, c, value):
        lower[lo * TILE : hi * TILE, c * TILE : (c + 1) * TILE] = value
        for ref, piece in zip(lp, split(value)):
            ref[lo * TILE : hi * TILE, c * TILE : (c + 1) * TILE] = piece

    shape = (TILE, TILE)
    eye = lax.broadcasted_iota(jnp.int32, shape, 0) == lax.broadcasted_iota(jnp.int32, shape, 1)

    def diagonal(j, known):
        block = times_t(feats(j, j + 1), feats(j, j + 1)) * scale + jnp.where(eye, DAMPING, 0.0)
        if known:
            block = block - times_t(lows(j, j + 1, known), lows(j, j + 1, known))
        return block

    for i in range(nb):
        for c in range(i + 1, nb):
            lower[i * TILE : (i + 1) * TILE, c * TILE : (c + 1) * TILE] = jnp.zeros(shape, f32)

    block, inverse = diagonal(0, 0), None
    for j in range(nb):
        if j >= 1 and j + 1 < nb:
            put(j + 1, nb, j - 1, times_t(split(panels[(j - 1) % 2, (j + 1) * TILE :, :]), inverse))
        if j + 1 < nb:
            panel = times_t(feats(j + 1, nb), feats(j, j + 1)) * scale
            if j:
                panel = panel - times_t(lows(j + 1, nb, j), lows(j, j + 1, j))
            panels[j % 2, (j + 1) * TILE :, :] = panel
            ahead = diagonal(j + 1, j)
        upper, inverse = factor_block([block[SUB * q : SUB * (q + 1), :] for q in range(TILE // SUB)])
        lower[j * TILE : (j + 1) * TILE, j * TILE : (j + 1) * TILE] = upper.T
        if j + 1 < nb:
            inverse = split(inverse)
            first = times_t(split(panels[j % 2, (j + 1) * TILE : (j + 2) * TILE, :]), inverse)
            put(j + 1, j + 2, j, first)
            first = split(first)
            block = ahead - times_t(first, first)

    height, width = out_ref.shape
    ex, param = place_ref[0], place_ref[1]
    per_tile = TILE // height
    taken = lower[pl.ds(pl.multiple_of(ex * width, width), width), pl.ds(pl.multiple_of(param // per_tile * TILE, TILE), TILE)]
    flipped = taken.T
    result = flipped[:height]
    for k in range(1, per_tile):
        result = jnp.where(param % per_tile == k, flipped[k * height : (k + 1) * height], result)
    out_ref[...] = result


def factor(place, own, other, examples, nb, block_shape):
    width = nb * TILE
    vmem = pl.BlockSpec(memory_space=pltpu.VMEM)
    return pl.pallas_call(
        factor_kernel,
        out_shape=jax.ShapeDtypeStruct(block_shape, f32),
        in_specs=[pl.BlockSpec(memory_space=pltpu.SMEM), vmem, vmem],
        out_specs=vmem,
        scratch_shapes=[pltpu.VMEM((width, width), f32), pltpu.VMEM((2, width, TILE), f32), pltpu.VMEM((examples, nb, TILE), f32)]
        + [pltpu.VMEM((width, examples), bf16)] * PIECES
        + [pltpu.VMEM((width, width), bf16)] * PIECES,
        compiler_params=pltpu.CompilerParams(vmem_limit_bytes=48 * 2**20),
        name="factor",
    )(place, own, other)


def per_device(
    ex_size, act_factor, grad_factor, proj_bank, tile_rows, tile_cols, tile_out, bank_left, bank_right, owner_map
):
    group = owner_map.shape[1]
    tokens, width = act_factor.shape
    seq_len = tokens // group
    out_tiles = 1024 // width
    ex, param = lax.axis_index("ex"), lax.axis_index("param")

    both = jnp.concatenate([f.reshape(group, seq_len, width) for f in (act_factor, grad_factor)], axis=1)
    both = lax.all_to_all(both, "param", split_axis=0, concat_axis=0, tiled=True)
    feats = project(
        both.reshape(2 * tokens, width),
        proj_bank,
        (tile_rows, tile_cols, tile_out, bank_left, bank_right),
        seq_len,
        out_tiles,
    )

    chips = ex_size // 2
    lines = [[2 * z + core for z in range(chips)] for core in range(2)]
    line = lax.all_to_all(
        jnp.broadcast_to(feats[None], (chips,) + feats.shape),
        "ex",
        split_axis=0,
        concat_axis=0,
        axis_index_groups=lines,
        tiled=True,
    )
    coded = encode(line)
    own = lax.all_to_all(
        jnp.broadcast_to(coded[None], (group,) + coded.shape), "param", split_axis=0, concat_axis=0, tiled=True
    )
    other = lax.ppermute(own, "ex", [(i, i ^ 1) for i in range(ex_size)])

    mine, at = owner_map[0, param], ex // 2
    taken = lax.dynamic_slice(own, (mine, at * out_tiles, 0), (1, out_tiles, width)).astype(f32)
    step = lax.dynamic_slice(own, (mine, chips * out_tiles + at, 0), (1, 1, width)).astype(f32)
    features = (taken * (jnp.exp2(step / STEPS) / LEVELS)).reshape(1, out_tiles * width)
    block = (out_tiles * width // group, out_tiles * width // ex_size)
    place = jnp.stack([ex, param]).astype(jnp.int32)
    r_block = factor(place, own, other, group * ex_size, out_tiles, block)
    return features, r_block


def solution(mesh):
    placed = (P("ex", "param"), P("ex", "param"), P(), P(), P(), P(), P(), P(), P("ex", None))
    return jax.shard_map(
        functools.partial(per_device, mesh.shape["ex"]),
        mesh=mesh,
        in_specs=placed,
        out_specs=(P(("ex", "param"), None), P("param", "ex")),
        check_vma=False,
    )
```

```python
import functools
import math

import jax
import jax.numpy as jnp
from jax import lax
from jax.experimental import pallas as pl
from jax.experimental.pallas import tpu as pltpu
from jax.sharding import PartitionSpec as P

TILE = 128
SUB = 8
DAMPING = 0.25
PIECES = 3
AHEAD = 4
TOGETHER = 4
LEVELS = 32767.0
STEPS = 16.0
f32, bf16 = jnp.float32, jnp.bfloat16


def project_kernel(
    seq_len, scale, rows_ref, cols_ref, outs_ref, lefts_ref, rights_ref, x_ref, bank_ref, feat_ref, table, acc
):
    banks = bank_ref.shape[0]
    for pair in range(banks // 2):
        tiles = jnp.concatenate([bank_ref[2 * pair], bank_ref[2 * pair + 1]], axis=1)
        both = jnp.dot(x_ref[...], tiles, preferred_element_type=f32)
        table[2 * pair] = both[:, :TILE]
        table[2 * pair + 1] = both[:, TILE:]
    acc[...] = jnp.zeros_like(acc)
    unroll = 8

    def add_slots(group, carry):
        for k in range(unroll):
            s = group * unroll + k
            left_at = pl.multiple_of(rows_ref[s] * (2 * seq_len), seq_len)
            right_at = pl.multiple_of(cols_ref[s] * (2 * seq_len) + seq_len, seq_len)
            left = table[lefts_ref[s], pl.ds(left_at, seq_len), :]
            right = table[rights_ref[s], pl.ds(right_at, seq_len), :]
            term = jnp.sum((left * right).reshape(seq_len // SUB, SUB, TILE), axis=0)
            acc[outs_ref[s]] += term
        return carry

    lax.fori_loop(0, rows_ref.shape[0] // unroll, add_slots, 0)
    feat_ref[...] = jnp.sum(acc[...], axis=1) * scale


def project(x, bank, ids, seq_len, out_tiles):
    scale = 1.0 / math.sqrt(seq_len * ids[0].shape[0] / out_tiles)
    smem = pl.BlockSpec(memory_space=pltpu.SMEM)
    vmem = pl.BlockSpec(memory_space=pltpu.VMEM)
    return pl.pallas_call(
        functools.partial(project_kernel, seq_len, scale),
        out_shape=jax.ShapeDtypeStruct((out_tiles, TILE), f32),
        in_specs=[smem] * 5 + [vmem] * 2,
        out_specs=vmem,
        scratch_shapes=[
            pltpu.VMEM((bank.shape[0], x.shape[0], TILE), f32),
            pltpu.VMEM((out_tiles, SUB, TILE), f32),
        ],
        compiler_params=pltpu.CompilerParams(vmem_limit_bytes=40 * 2**20),
        name="project",
    )(*ids, x, bank)


def factor_block(rows):
    groups = len(rows)
    lane = lax.broadcasted_iota(jnp.int32, (SUB, TILE), 1)
    sub = lax.broadcasted_iota(jnp.int32, (SUB, TILE), 0)
    rows = list(rows)

    def column(p, c):
        return jnp.broadcast_to(rows[p][:, c : c + 1], (SUB, TILE))

    def entry(x, s):
        return jnp.broadcast_to(x[s : s + 1, :], (SUB, TILE))

    def wanted(i, first):
        for c in range(max(i, 0), min(TILE, i + SUB + 1)):
            for p in range(first, groups):
                if c <= i + AHEAD or p <= c // SUB:
                    yield c, p

    spread = {(c, p): column(p, c) for c, p in wanted(-1, 0)}
    small, upper, inverse_lower = {}, [], []
    for i in range(TILE):
        q, s = divmod(i, SUB)
        if s == 0:
            small = {(k, l): entry(spread[SUB * q + l, q], k) for k in range(SUB) for l in range(k, SUB)}
            root = None
        if s % TOGETHER == 0:
            held = range(s, s + TOGETHER)
            full = {k: entry(rows[q], k) for k in held}
            across = {(k, c): entry(spread[c, q], k) for k in held for c in {c for c, _ in spread if c >= SUB * (q + 1)}}
        inverse = 1.0 / small[s, s]
        one_root = lax.rsqrt(small[s, s])
        root = one_root if root is None else jnp.where(sub == s, one_root, root)
        weights = {SUB * q + l: small[s, l] * inverse for l in range(s + 1, SUB)}
        at_pivot, below = lane == i, sub > s
        row = jnp.where(at_pivot, 1.0, full[s]) * inverse
        later = [k for k in held if k > s]
        for k in later:
            full[k] = jnp.where(at_pivot, 0.0, full[k]) - small[s, k] * row
        for c in sorted({c for c, _ in spread if c >= SUB * (q + 1)}):
            value = across[s, c] if (s, c) in across else entry(spread[c, q], s)
            weights[c] = value * inverse
            for k in later:
                if (k, c) in across:
                    across[k, c] = across[k, c] - small[s, k] * weights[c]
        for l in range(s + 1, SUB):
            for m in range(l, SUB):
                small[l, m] = small[l, m] - small[s, m] * weights[SUB * q + l]
        own = jnp.where(below, spread[i, q], 0.0)
        for c in sorted({c for c, _ in spread if c > i}):
            for p in range(q, groups):
                if (c, p) in spread:
                    spread[c, p] = spread[c, p] - (own if p == q else spread[i, p]) * weights[c]
        if s < SUB - 1:
            rows[q] = jnp.where(at_pivot & below, 0.0, rows[q]) - own * row
        for p in range(q + 1, groups):
            rows[p] = jnp.where(at_pivot, 0.0, rows[p]) - spread[i, p] * row
        if s == SUB - 1:
            r = sub + SUB * q
            upper.append(jnp.where(lane >= r, rows[q], 0.0) * root)
            inverse_lower.append(jnp.where(lane < r, rows[q], jnp.where(lane == r, 1.0, 0.0)) * root)
        first = (i + 1) // SUB
        spread = {(c, p): v for (c, p), v in spread.items() if c > i and p >= first}
        for c, p in wanted(i, first):
            if c > i and (c, p) not in spread:
                spread[c, p] = column(p, c)
    return jnp.concatenate(upper, 0), jnp.concatenate(inverse_lower, 0)


def split(x):
    pieces = []
    for k in range(PIECES):
        piece = x.astype(bf16)
        pieces.append(piece)
        if k < PIECES - 1:
            x = x - piece.astype(f32)
    return pieces


def times_t(a, b):
    total = None
    for i, k in sorted(((i, k) for i in range(PIECES) for k in range(PIECES) if i + k < max(PIECES, 3)), key=lambda ik: -sum(ik)):
        term = lax.dot_general(a[i], b[k], (((1,), (1,)), ((), ())), preferred_element_type=f32)
        total = term if total is None else total + term
    return total


def encode(rows):
    count, blocks, width = rows.shape
    top = jnp.max(jnp.abs(rows), axis=(1, 2), keepdims=True)
    step = jnp.ceil(STEPS * jnp.log2(jnp.maximum(top, 1e-30)))
    coded = jnp.clip(jnp.round(rows * (LEVELS * jnp.exp2(step / -STEPS))), -LEVELS, LEVELS)
    scales = jnp.broadcast_to(step[:, 0], (count, width))
    parts = [coded.reshape(count * blocks, width), scales, jnp.zeros((-count % 16, width), f32)]
    return jnp.concatenate(parts, axis=0).astype(jnp.int16)


def factor_kernel(place_ref, owners_ref, own_ref, other_ref, features_ref, out_ref, lower, panels, feat, *pieces):
    ft, lp = pieces[:PIECES], pieces[PIECES:]
    examples, nb, _ = feat.shape
    peers = own_ref.shape[0]
    count = examples // (2 * peers)
    scale = 1.0 / examples
    for h, ref in enumerate((own_ref, other_ref)):

        def decode(peer, carry):
            coded = ref[peer].astype(jnp.int32).astype(f32)
            steps = coded[count * nb : count * nb + count]
            scales = jnp.exp2(steps * (1.0 / STEPS)) * (1.0 / LEVELS)
            values = coded[: count * nb].reshape(count, nb, TILE) * jnp.broadcast_to(scales[:, None, :], (count, nb, TILE))
            feat[pl.ds(h * peers * count + peer * count, count)] = values
            return carry

        lax.fori_loop(0, peers, decode, 0)
    height, width = out_ref.shape
    ex, param = place_ref[0], place_ref[1]
    mine = feat[owners_ref[0, param] * count + ex // 2]
    for b in range(nb):
        features_ref[:, b * TILE : (b + 1) * TILE] = mine[b : b + 1]

    def turn(b):
        for k, piece in enumerate(split(feat[:, b, :].T)):
            ft[k][b * TILE : (b + 1) * TILE, :] = piece


    def feats(lo, hi):
        return [ref[lo * TILE : hi * TILE, :] for ref in ft]

    def lows(lo, hi, to):
        return [ref[lo * TILE : hi * TILE, : to * TILE] for ref in lp]

    def put(lo, hi, c, value):
        lower[lo * TILE : hi * TILE, c * TILE : (c + 1) * TILE] = value
        for ref, piece in zip(lp, split(value)):
            ref[lo * TILE : hi * TILE, c * TILE : (c + 1) * TILE] = piece

    shape = (TILE, TILE)
    eye = lax.broadcasted_iota(jnp.int32, shape, 0) == lax.broadcasted_iota(jnp.int32, shape, 1)

    def diagonal(j, known):
        block = times_t(feats(j, j + 1), feats(j, j + 1)) * scale + jnp.where(eye, DAMPING, 0.0)
        if known:
            block = block - times_t(lows(j, j + 1, known), lows(j, j + 1, known))
        return block

    turn(0)
    block, inverse = diagonal(0, 0), None
    for b in range(1, nb):
        turn(b)
    for i in range(nb):
        for c in range(i + 1, nb):
            lower[i * TILE : (i + 1) * TILE, c * TILE : (c + 1) * TILE] = jnp.zeros(shape, f32)

    for j in range(nb):
        if j >= 1 and j + 1 < nb:
            put(j + 1, nb, j - 1, times_t(split(panels[(j - 1) % 2, (j + 1) * TILE :, :]), inverse))
        if j + 1 < nb:
            panel = times_t(feats(j + 1, nb), feats(j, j + 1)) * scale
            if j:
                panel = panel - times_t(lows(j + 1, nb, j), lows(j, j + 1, j))
            panels[j % 2, (j + 1) * TILE :, :] = panel
            ahead = diagonal(j + 1, j)
        upper, inverse = factor_block([block[SUB * q : SUB * (q + 1), :] for q in range(TILE // SUB)])
        lower[j * TILE : (j + 1) * TILE, j * TILE : (j + 1) * TILE] = upper.T
        if j + 1 < nb:
            inverse = split(inverse)
            first = times_t(split(panels[j % 2, (j + 1) * TILE : (j + 2) * TILE, :]), inverse)
            put(j + 1, j + 2, j, first)
            first = split(first)
            block = ahead - times_t(first, first)

    per_tile = TILE // height
    taken = lower[pl.ds(pl.multiple_of(ex * width, width), width), pl.ds(pl.multiple_of(param // per_tile * TILE, TILE), TILE)]
    flipped = taken.T
    result = flipped[:height]
    for k in range(1, per_tile):
        result = jnp.where(param % per_tile == k, flipped[k * height : (k + 1) * height], result)
    out_ref[...] = result


def factor(place, owners, own, other, examples, nb, block_shape):
    width = nb * TILE
    smem = pl.BlockSpec(memory_space=pltpu.SMEM)
    vmem = pl.BlockSpec(memory_space=pltpu.VMEM)
    return pl.pallas_call(
        factor_kernel,
        out_shape=(jax.ShapeDtypeStruct((1, width), f32), jax.ShapeDtypeStruct(block_shape, f32)),
        in_specs=[smem, smem, vmem, vmem],
        out_specs=(vmem, vmem),
        scratch_shapes=[pltpu.VMEM((width, width), f32), pltpu.VMEM((2, width, TILE), f32), pltpu.VMEM((examples, nb, TILE), f32)]
        + [pltpu.VMEM((width, examples), bf16)] * PIECES
        + [pltpu.VMEM((width, width), bf16)] * PIECES,
        compiler_params=pltpu.CompilerParams(vmem_limit_bytes=48 * 2**20),
        name="factor",
    )(place, owners, own, other)


def per_device(
    ex_size, act_factor, grad_factor, proj_bank, tile_rows, tile_cols, tile_out, bank_left, bank_right, owner_map
):
    group = owner_map.shape[1]
    tokens, width = act_factor.shape
    seq_len = tokens // group
    out_tiles = 1024 // width
    ex, param = lax.axis_index("ex"), lax.axis_index("param")

    both = jnp.concatenate([f.reshape(group, seq_len, width) for f in (act_factor, grad_factor)], axis=1)
    both = lax.all_to_all(both, "param", split_axis=0, concat_axis=0, tiled=True)
    feats = project(
        both.reshape(2 * tokens, width),
        proj_bank,
        (tile_rows, tile_cols, tile_out, bank_left, bank_right),
        seq_len,
        out_tiles,
    )

    chips = ex_size // 2
    lines = [[2 * z + core for z in range(chips)] for core in range(2)]
    line = lax.all_to_all(
        jnp.broadcast_to(feats[None], (chips,) + feats.shape),
        "ex",
        split_axis=0,
        concat_axis=0,
        axis_index_groups=lines,
        tiled=True,
    )
    coded = encode(line)
    own = lax.all_to_all(
        jnp.broadcast_to(coded[None], (group,) + coded.shape), "param", split_axis=0, concat_axis=0, tiled=True
    )
    other = lax.ppermute(own, "ex", [(i, i ^ 1) for i in range(ex_size)])

    block = (out_tiles * width // group, out_tiles * width // ex_size)
    place = jnp.stack([ex, param]).astype(jnp.int32)
    return factor(place, owner_map, own, other, group * ex_size, out_tiles, block)


def solution(mesh):
    placed = (P("ex", "param"), P("ex", "param"), P(), P(), P(), P(), P(), P(), P("ex", None))
    return jax.shard_map(
        functools.partial(per_device, mesh.shape["ex"]),
        mesh=mesh,
        in_specs=placed,
        out_specs=(P(("ex", "param"), None), P("param", "ex")),
        check_vma=False,
    )
```

```python
import functools
import math

import jax
import jax.numpy as jnp
from jax import lax
from jax.experimental import pallas as pl
from jax.experimental.pallas import tpu as pltpu
from jax.sharding import PartitionSpec as P

TILE = 128
SUB = 8
DAMPING = 0.25
PIECES = 3
AHEAD = 5
DEEP = 10
LEVELS = 32767.0
STEPS = 16.0
f32, bf16 = jnp.float32, jnp.bfloat16


def project_kernel(
    seq_len, scale, rows_ref, cols_ref, outs_ref, lefts_ref, rights_ref, x_ref, bank_ref, feat_ref, table, acc
):
    banks = bank_ref.shape[0]
    for pair in range(banks // 2):
        tiles = jnp.concatenate([bank_ref[2 * pair], bank_ref[2 * pair + 1]], axis=1)
        both = jnp.dot(x_ref[...], tiles, preferred_element_type=f32)
        table[2 * pair] = both[:, :TILE]
        table[2 * pair + 1] = both[:, TILE:]
    acc[...] = jnp.zeros_like(acc)
    unroll = 8

    def add_slots(group, carry):
        for k in range(unroll):
            s = group * unroll + k
            left_at = pl.multiple_of(rows_ref[s] * (2 * seq_len), seq_len)
            right_at = pl.multiple_of(cols_ref[s] * (2 * seq_len) + seq_len, seq_len)
            left = table[lefts_ref[s], pl.ds(left_at, seq_len), :]
            right = table[rights_ref[s], pl.ds(right_at, seq_len), :]
            term = jnp.sum((left * right).reshape(seq_len // SUB, SUB, TILE), axis=0)
            acc[outs_ref[s]] += term
        return carry

    lax.fori_loop(0, rows_ref.shape[0] // unroll, add_slots, 0)
    feat_ref[...] = jnp.broadcast_to((jnp.sum(acc[...], axis=1) * scale)[None], feat_ref.shape)


def project(x, bank, ids, seq_len, out_tiles, copies):
    scale = 1.0 / math.sqrt(seq_len * ids[0].shape[0] / out_tiles)
    smem = pl.BlockSpec(memory_space=pltpu.SMEM)
    vmem = pl.BlockSpec(memory_space=pltpu.VMEM)
    return pl.pallas_call(
        functools.partial(project_kernel, seq_len, scale),
        out_shape=jax.ShapeDtypeStruct((copies, out_tiles, TILE), f32),
        in_specs=[smem] * 5 + [vmem] * 2,
        out_specs=vmem,
        scratch_shapes=[
            pltpu.VMEM((bank.shape[0], x.shape[0], TILE), f32),
            pltpu.VMEM((out_tiles, SUB, TILE), f32),
        ],
        compiler_params=pltpu.CompilerParams(vmem_limit_bytes=40 * 2**20),
        name="project",
    )(*ids, x, bank)


def factor_block(rows):
    groups = len(rows)
    lane = lax.broadcasted_iota(jnp.int32, (SUB, TILE), 1)
    sub = lax.broadcasted_iota(jnp.int32, (SUB, TILE), 0)
    rows = list(rows)

    def column(p, c):
        return jnp.broadcast_to(rows[p][:, c : c + 1], (SUB, TILE))

    def entry(x, s):
        return jnp.broadcast_to(x[s : s + 1, :], (SUB, TILE))

    def wanted(i, first):
        for c in range(max(i, 0), min(TILE, i + DEEP + 1)):
            for p in range(first, groups):
                if c <= i + AHEAD or p <= c // SUB:
                    yield c, p

    spread = {(c, p): column(p, c) for c, p in wanted(-1, 0)}
    upper, inverse_lower = [], []
    for i in range(TILE):
        q, s = divmod(i, SUB)
        pivot = entry(spread[i, q], s)
        inverse, one_root = 1.0 / pivot, lax.rsqrt(pivot)
        root = one_root if s == 0 else jnp.where(sub == s, one_root, root)
        at_pivot, below = lane == i, sub > s
        row = jnp.where(at_pivot, 1.0, entry(rows[q], s)) * inverse
        own = jnp.where(below, spread[i, q], 0.0)
        for c in sorted({c for c, _ in spread if c > i}):
            weight = entry(spread[c, q], s) * inverse
            for p in range(q if s < SUB - 1 else q + 1, groups):
                if (c, p) in spread:
                    spread[c, p] = spread[c, p] - (own if p == q else spread[i, p]) * weight
        if s < SUB - 1:
            rows[q] = jnp.where(at_pivot & below, 0.0, rows[q]) - own * row
        for p in range(q + 1, groups):
            rows[p] = jnp.where(at_pivot, 0.0, rows[p]) - spread[i, p] * row
        if s == SUB - 1:
            r = sub + SUB * q
            upper.append(jnp.where(lane >= r, rows[q], 0.0) * root)
            inverse_lower.append(jnp.where(lane < r, rows[q], jnp.where(lane == r, 1.0, 0.0)) * root)
        first = (i + 1) // SUB
        spread = {(c, p): v for (c, p), v in spread.items() if c > i and p >= first}
        for c, p in wanted(i, first):
            if c > i and (c, p) not in spread:
                spread[c, p] = column(p, c)
    return jnp.concatenate(upper, 0), jnp.concatenate(inverse_lower, 0)


def split(x):
    pieces = []
    for k in range(PIECES):
        piece = x.astype(bf16)
        pieces.append(piece)
        if k < PIECES - 1:
            x = x - piece.astype(f32)
    return pieces


def times_t(a, b):
    total = None
    for i, k in sorted(((i, k) for i in range(PIECES) for k in range(PIECES) if i + k < max(PIECES, 3)), key=lambda ik: -sum(ik)):
        term = lax.dot_general(a[i], b[k], (((1,), (1,)), ((), ())), preferred_element_type=f32)
        total = term if total is None else total + term
    return total


def encode(rows):
    count, blocks, width = rows.shape
    top = jnp.max(jnp.abs(rows), axis=(1, 2), keepdims=True)
    step = jnp.ceil(STEPS * jnp.log2(jnp.maximum(top, 1e-30)))
    coded = jnp.clip(jnp.round(rows * (LEVELS * jnp.exp2(step / -STEPS))), -LEVELS, LEVELS)
    scales = jnp.broadcast_to(step[:, 0], (count, width))
    parts = [coded.reshape(count * blocks, width), scales, jnp.zeros((-count % SUB, width), f32)]
    return jnp.concatenate(parts, axis=0).astype(jnp.int16)


def factor_kernel(place_ref, owners_ref, own_ref, other_ref, features_ref, out_ref, lower, panels, feat, *pieces):
    ft, lp = pieces[:PIECES], pieces[PIECES:]
    examples, nb, _ = feat.shape
    peers = own_ref.shape[0]
    count = examples // (2 * peers)
    scale = 1.0 / examples
    for h, ref in enumerate((own_ref, other_ref)):

        def decode(peer, carry):
            coded = ref[peer].astype(jnp.int32).astype(f32)
            steps = coded[count * nb : count * nb + count]
            scales = jnp.exp2(steps * (1.0 / STEPS)) * (1.0 / LEVELS)
            values = coded[: count * nb].reshape(count, nb, TILE) * jnp.broadcast_to(scales[:, None, :], (count, nb, TILE))
            feat[pl.ds(h * peers * count + peer * count, count)] = values
            return carry

        lax.fori_loop(0, peers, decode, 0, unroll=4)
    height, width = out_ref.shape
    ex, param = place_ref[0], place_ref[1]
    mine = feat[owners_ref[0, param] * count + ex // 2]
    for b in range(nb):
        features_ref[:, b * TILE : (b + 1) * TILE] = mine[b : b + 1]

    def turn(b):
        for k, piece in enumerate(split(feat[:, b, :].T)):
            ft[k][b * TILE : (b + 1) * TILE, :] = piece


    def feats(lo, hi):
        return [ref[lo * TILE : hi * TILE, :] for ref in ft]

    def lows(lo, hi, to):
        return [ref[lo * TILE : hi * TILE, : to * TILE] for ref in lp]

    def put(lo, hi, c, value):
        lower[lo * TILE : hi * TILE, c * TILE : (c + 1) * TILE] = value
        for ref, piece in zip(lp, split(value)):
            ref[lo * TILE : hi * TILE, c * TILE : (c + 1) * TILE] = piece

    shape = (TILE, TILE)
    eye = lax.broadcasted_iota(jnp.int32, shape, 0) == lax.broadcasted_iota(jnp.int32, shape, 1)

    def diagonal(j, known):
        block = times_t(feats(j, j + 1), feats(j, j + 1)) * scale + jnp.where(eye, DAMPING, 0.0)
        if known:
            block = block - times_t(lows(j, j + 1, known), lows(j, j + 1, known))
        return block

    turn(0)
    block, inverse = diagonal(0, 0), None
    for b in range(1, nb):
        turn(b)
    for i in range(nb):
        for c in range(i + 1, nb):
            lower[i * TILE : (i + 1) * TILE, c * TILE : (c + 1) * TILE] = jnp.zeros(shape, f32)

    for j in range(nb):
        if j >= 1 and j + 1 < nb:
            put(j + 1, nb, j - 1, times_t(split(panels[(j - 1) % 2, (j + 1) * TILE :, :]), inverse))
        if j + 1 < nb:
            panel = times_t(feats(j + 1, nb), feats(j, j + 1)) * scale
            if j:
                panel = panel - times_t(lows(j + 1, nb, j), lows(j, j + 1, j))
            panels[j % 2, (j + 1) * TILE :, :] = panel
            ahead = diagonal(j + 1, j)
        upper, inverse = factor_block([block[SUB * q : SUB * (q + 1), :] for q in range(TILE // SUB)])
        lower[j * TILE : (j + 1) * TILE, j * TILE : (j + 1) * TILE] = upper.T
        if j + 1 < nb:
            inverse = split(inverse)
            first = times_t(split(panels[j % 2, (j + 1) * TILE : (j + 2) * TILE, :]), inverse)
            put(j + 1, j + 2, j, first)
            first = split(first)
            block = ahead - times_t(first, first)

    per_tile = TILE // height
    taken = lower[pl.ds(pl.multiple_of(ex * width, width), width), pl.ds(pl.multiple_of(param // per_tile * TILE, TILE), TILE)]
    flipped = taken.T
    result = flipped[:height]
    for k in range(1, per_tile):
        result = jnp.where(param % per_tile == k, flipped[k * height : (k + 1) * height], result)
    out_ref[...] = result


def factor(place, owners, own, other, examples, nb, block_shape):
    width = nb * TILE
    smem = pl.BlockSpec(memory_space=pltpu.SMEM)
    vmem = pl.BlockSpec(memory_space=pltpu.VMEM)
    return pl.pallas_call(
        factor_kernel,
        out_shape=(jax.ShapeDtypeStruct((1, width), f32), jax.ShapeDtypeStruct(block_shape, f32)),
        in_specs=[smem, smem, vmem, vmem],
        out_specs=(vmem, vmem),
        scratch_shapes=[pltpu.VMEM((width, width), f32), pltpu.VMEM((2, width, TILE), f32), pltpu.VMEM((examples, nb, TILE), f32)]
        + [pltpu.VMEM((width, examples), bf16)] * PIECES
        + [pltpu.VMEM((width, width), bf16)] * PIECES,
        compiler_params=pltpu.CompilerParams(vmem_limit_bytes=48 * 2**20),
        name="factor",
    )(place, owners, own, other)


def per_device(
    ex_size, act_factor, grad_factor, proj_bank, tile_rows, tile_cols, tile_out, bank_left, bank_right, owner_map
):
    group = owner_map.shape[1]
    tokens, width = act_factor.shape
    seq_len = tokens // group
    out_tiles = 1024 // width
    ex, param = lax.axis_index("ex"), lax.axis_index("param")

    both = jnp.concatenate([f.reshape(group, seq_len, width) for f in (act_factor, grad_factor)], axis=1)
    both = lax.all_to_all(both, "param", split_axis=0, concat_axis=0, tiled=True)
    feats = project(
        both.reshape(2 * tokens, width),
        proj_bank,
        (tile_rows, tile_cols, tile_out, bank_left, bank_right),
        seq_len,
        out_tiles,
        ex_size // 2,
    )

    chips = ex_size // 2
    lines = [[2 * z + core for z in range(chips)] for core in range(2)]
    line = lax.all_to_all(
        feats,
        "ex",
        split_axis=0,
        concat_axis=0,
        axis_index_groups=lines,
        tiled=True,
    )
    coded = encode(line)
    own = lax.all_to_all(
        jnp.broadcast_to(coded[None], (group,) + coded.shape), "param", split_axis=0, concat_axis=0, tiled=True
    )
    other = lax.ppermute(own, "ex", [(i, i ^ 1) for i in range(ex_size)])

    block = (out_tiles * width // group, out_tiles * width // ex_size)
    place = jnp.stack([ex, param]).astype(jnp.int32)
    return factor(place, owner_map, own, other, group * ex_size, out_tiles, block)


def solution(mesh):
    placed = (P("ex", "param"), P("ex", "param"), P(), P(), P(), P(), P(), P(), P("ex", None))
    return jax.shard_map(
        functools.partial(per_device, mesh.shape["ex"]),
        mesh=mesh,
        in_specs=placed,
        out_specs=(P(("ex", "param"), None), P("param", "ex")),
        check_vma=False,
    )
```

```python
import functools
import math

import jax
import jax.numpy as jnp
from jax import lax
from jax.experimental import pallas as pl
from jax.experimental.pallas import tpu as pltpu
from jax.sharding import PartitionSpec as P

TILE = 128
SUB = 8
DAMPING = 0.25
PIECES = 3
AHEAD = 5
DEEP = 10
LEVELS = 32767.0
STEPS = 16.0
f32, bf16 = jnp.float32, jnp.bfloat16


def project_kernel(
    seq_len, scale, rows_in, cols_in, outs_in, lefts_in, rights_in, x_ref, bank_ref, feat_ref, table, acc, *held
):
    lists, arrived = held[:-1], held[-1]
    copies = [
        pltpu.make_async_copy(source, target, arrived.at[k])
        for k, (source, target) in enumerate(zip((rows_in, cols_in, outs_in, lefts_in, rights_in), lists))
    ]
    for copy in copies:
        copy.start()
    rows_ref, cols_ref, outs_ref, lefts_ref, rights_ref = lists
    banks = bank_ref.shape[0]
    for pair in range(banks // 2):
        tiles = jnp.concatenate([bank_ref[2 * pair], bank_ref[2 * pair + 1]], axis=1)
        both = jnp.dot(x_ref[...], tiles, preferred_element_type=f32)
        table[2 * pair] = both[:, :TILE]
        table[2 * pair + 1] = both[:, TILE:]
    acc[...] = jnp.zeros_like(acc)
    for copy in copies:
        copy.wait()
    unroll = 8

    def add_slots(group, carry):
        for k in range(unroll):
            s = group * unroll + k
            left_at = pl.multiple_of(rows_ref[s] * (2 * seq_len), seq_len)
            right_at = pl.multiple_of(cols_ref[s] * (2 * seq_len) + seq_len, seq_len)
            left = table[lefts_ref[s], pl.ds(left_at, seq_len), :]
            right = table[rights_ref[s], pl.ds(right_at, seq_len), :]
            term = jnp.sum((left * right).reshape(seq_len // SUB, SUB, TILE), axis=0)
            acc[outs_ref[s]] += term
        return carry

    lax.fori_loop(0, rows_ref.shape[0] // unroll, add_slots, 0)
    feat_ref[...] = jnp.broadcast_to((jnp.sum(acc[...], axis=1) * scale)[None], feat_ref.shape)


def project(x, bank, ids, seq_len, out_tiles, copies):
    scale = 1.0 / math.sqrt(seq_len * ids[0].shape[0] / out_tiles)
    left = pl.BlockSpec(memory_space=pl.ANY)
    vmem = pl.BlockSpec(memory_space=pltpu.VMEM)
    return pl.pallas_call(
        functools.partial(project_kernel, seq_len, scale),
        out_shape=jax.ShapeDtypeStruct((copies, out_tiles, TILE), f32),
        in_specs=[left] * 5 + [vmem] * 2,
        out_specs=vmem,
        scratch_shapes=[
            pltpu.VMEM((bank.shape[0], x.shape[0], TILE), f32),
            pltpu.VMEM((out_tiles, SUB, TILE), f32),
        ]
        + [pltpu.SMEM(ids[0].shape, jnp.int32)] * 5
        + [pltpu.SemaphoreType.DMA((5,))],
        compiler_params=pltpu.CompilerParams(vmem_limit_bytes=40 * 2**20),
        name="project",
    )(*ids, x, bank)


def factor_block(rows):
    groups = len(rows)
    lane = lax.broadcasted_iota(jnp.int32, (SUB, TILE), 1)
    sub = lax.broadcasted_iota(jnp.int32, (SUB, TILE), 0)
    rows = list(rows)

    def column(p, c):
        return jnp.broadcast_to(rows[p][:, c : c + 1], (SUB, TILE))

    def entry(x, s):
        return jnp.broadcast_to(x[s : s + 1, :], (SUB, TILE))

    def wanted(i, first):
        for c in range(max(i, 0), min(TILE, i + DEEP + 1)):
            for p in range(first, groups):
                if c <= i + AHEAD or p <= c // SUB:
                    yield c, p

    spread = {(c, p): column(p, c) for c, p in wanted(-1, 0)}
    upper, inverse_lower = [], []
    for i in range(TILE):
        q, s = divmod(i, SUB)
        pivot = entry(spread[i, q], s)
        inverse, one_root = 1.0 / pivot, lax.rsqrt(pivot)
        root = one_root if s == 0 else jnp.where(sub == s, one_root, root)
        at_pivot, below = lane == i, sub > s
        row = jnp.where(at_pivot, 1.0, entry(rows[q], s)) * inverse
        own = jnp.where(below, spread[i, q], 0.0)
        for c in sorted({c for c, _ in spread if c > i}):
            weight = entry(spread[c, q], s) * inverse
            for p in range(q if s < SUB - 1 else q + 1, groups):
                if (c, p) in spread:
                    spread[c, p] = spread[c, p] - (own if p == q else spread[i, p]) * weight
        if s < SUB - 1:
            rows[q] = jnp.where(at_pivot & below, 0.0, rows[q]) - own * row
        for p in range(q + 1, groups):
            rows[p] = jnp.where(at_pivot, 0.0, rows[p]) - spread[i, p] * row
        if s == SUB - 1:
            r = sub + SUB * q
            upper.append(jnp.where(lane >= r, rows[q], 0.0) * root)
            inverse_lower.append(jnp.where(lane < r, rows[q], jnp.where(lane == r, 1.0, 0.0)) * root)
        first = (i + 1) // SUB
        spread = {(c, p): v for (c, p), v in spread.items() if c > i and p >= first}
        for c, p in wanted(i, first):
            if c > i and (c, p) not in spread:
                spread[c, p] = column(p, c)
    return jnp.concatenate(upper, 0), jnp.concatenate(inverse_lower, 0)


def split(x):
    pieces = []
    for k in range(PIECES):
        piece = x.astype(bf16)
        pieces.append(piece)
        if k < PIECES - 1:
            x = x - piece.astype(f32)
    return pieces


def times_t(a, b):
    total = None
    for i, k in sorted(((i, k) for i in range(PIECES) for k in range(PIECES) if i + k < max(PIECES, 3)), key=lambda ik: -sum(ik)):
        term = lax.dot_general(a[i], b[k], (((1,), (1,)), ((), ())), preferred_element_type=f32)
        total = term if total is None else total + term
    return total


def encode(rows):
    count, blocks, width = rows.shape
    top = jnp.max(jnp.abs(rows), axis=(1, 2), keepdims=True)
    step = jnp.ceil(STEPS * jnp.log2(jnp.maximum(top, 1e-30)))
    coded = jnp.clip(jnp.round(rows * (LEVELS * jnp.exp2(step / -STEPS))), -LEVELS, LEVELS)
    scales = jnp.broadcast_to(step[:, 0], (count, width))
    parts = [coded.reshape(count * blocks, width), scales, jnp.zeros((-count % SUB, width), f32)]
    return jnp.concatenate(parts, axis=0).astype(jnp.int16)


def factor_kernel(place_ref, owners_ref, own_ref, other_ref, features_ref, out_ref, lower, panels, feat, *pieces):
    ft, lp = pieces[:PIECES], pieces[PIECES:]
    examples, nb, _ = feat.shape
    peers = own_ref.shape[0]
    count = examples // (2 * peers)
    scale = 1.0 / examples
    for h, ref in enumerate((own_ref, other_ref)):

        def decode(peer, carry):
            coded = ref[peer].astype(jnp.int32).astype(f32)
            steps = coded[count * nb : count * nb + count]
            scales = jnp.exp2(steps * (1.0 / STEPS)) * (1.0 / LEVELS)
            values = coded[: count * nb].reshape(count, nb, TILE) * jnp.broadcast_to(scales[:, None, :], (count, nb, TILE))
            feat[pl.ds(h * peers * count + peer * count, count)] = values
            return carry

        lax.fori_loop(0, peers, decode, 0, unroll=8)
    height, width = out_ref.shape
    ex, param = place_ref[0], place_ref[1]
    mine = feat[owners_ref[0, param] * count + ex // 2]
    for b in range(nb):
        features_ref[:, b * TILE : (b + 1) * TILE] = mine[b : b + 1]

    def turn(b):
        for k, piece in enumerate(split(feat[:, b, :].T)):
            ft[k][b * TILE : (b + 1) * TILE, :] = piece


    def feats(lo, hi):
        return [ref[lo * TILE : hi * TILE, :] for ref in ft]

    def lows(lo, hi, to):
        return [ref[lo * TILE : hi * TILE, : to * TILE] for ref in lp]

    def put(lo, hi, c, value):
        lower[lo * TILE : hi * TILE, c * TILE : (c + 1) * TILE] = value
        for ref, piece in zip(lp, split(value)):
            ref[lo * TILE : hi * TILE, c * TILE : (c + 1) * TILE] = piece

    shape = (TILE, TILE)
    eye = lax.broadcasted_iota(jnp.int32, shape, 0) == lax.broadcasted_iota(jnp.int32, shape, 1)

    def diagonal(j, known):
        block = times_t(feats(j, j + 1), feats(j, j + 1)) * scale + jnp.where(eye, DAMPING, 0.0)
        if known:
            block = block - times_t(lows(j, j + 1, known), lows(j, j + 1, known))
        return block

    turn(0)
    block, inverse = diagonal(0, 0), None
    for b in range(1, nb):
        turn(b)
    for i in range(nb):
        for c in range(i + 1, nb):
            lower[i * TILE : (i + 1) * TILE, c * TILE : (c + 1) * TILE] = jnp.zeros(shape, f32)

    for j in range(nb):
        if j >= 1 and j + 1 < nb:
            put(j + 1, nb, j - 1, times_t(split(panels[(j - 1) % 2, (j + 1) * TILE :, :]), inverse))
        if j + 1 < nb:
            panel = times_t(feats(j + 1, nb), feats(j, j + 1)) * scale
            if j:
                panel = panel - times_t(lows(j + 1, nb, j), lows(j, j + 1, j))
            panels[j % 2, (j + 1) * TILE :, :] = panel
            ahead = diagonal(j + 1, j)
        upper, inverse = factor_block([block[SUB * q : SUB * (q + 1), :] for q in range(TILE // SUB)])
        lower[j * TILE : (j + 1) * TILE, j * TILE : (j + 1) * TILE] = upper.T
        if j + 1 < nb:
            inverse = split(inverse)
            first = times_t(split(panels[j % 2, (j + 1) * TILE : (j + 2) * TILE, :]), inverse)
            put(j + 1, j + 2, j, first)
            first = split(first)
            block = ahead - times_t(first, first)

    per_tile = TILE // height
    taken = lower[pl.ds(pl.multiple_of(ex * width, width), width), pl.ds(pl.multiple_of(param // per_tile * TILE, TILE), TILE)]
    flipped = taken.T
    result = flipped[:height]
    for k in range(1, per_tile):
        result = jnp.where(param % per_tile == k, flipped[k * height : (k + 1) * height], result)
    out_ref[...] = result


def factor(place, owners, own, other, examples, nb, block_shape):
    width = nb * TILE
    smem = pl.BlockSpec(memory_space=pltpu.SMEM)
    vmem = pl.BlockSpec(memory_space=pltpu.VMEM)
    return pl.pallas_call(
        factor_kernel,
        out_shape=(jax.ShapeDtypeStruct((1, width), f32), jax.ShapeDtypeStruct(block_shape, f32)),
        in_specs=[smem, smem, vmem, vmem],
        out_specs=(vmem, vmem),
        scratch_shapes=[pltpu.VMEM((width, width), f32), pltpu.VMEM((2, width, TILE), f32), pltpu.VMEM((examples, nb, TILE), f32)]
        + [pltpu.VMEM((width, examples), bf16)] * PIECES
        + [pltpu.VMEM((width, width), bf16)] * PIECES,
        compiler_params=pltpu.CompilerParams(vmem_limit_bytes=48 * 2**20),
        name="factor",
    )(place, owners, own, other)


def per_device(
    ex_size, act_factor, grad_factor, proj_bank, tile_rows, tile_cols, tile_out, bank_left, bank_right, owner_map
):
    group = owner_map.shape[1]
    tokens, width = act_factor.shape
    seq_len = tokens // group
    out_tiles = 1024 // width
    ex, param = lax.axis_index("ex"), lax.axis_index("param")

    both = jnp.concatenate([f.reshape(group, seq_len, width) for f in (act_factor, grad_factor)], axis=1)
    both = lax.all_to_all(both, "param", split_axis=0, concat_axis=0, tiled=True)
    feats = project(
        both.reshape(2 * tokens, width),
        proj_bank,
        (tile_rows, tile_cols, tile_out, bank_left, bank_right),
        seq_len,
        out_tiles,
        ex_size // 2,
    )

    chips = ex_size // 2
    lines = [[2 * z + core for z in range(chips)] for core in range(2)]
    line = lax.all_to_all(
        feats,
        "ex",
        split_axis=0,
        concat_axis=0,
        axis_index_groups=lines,
        tiled=True,
    )
    coded = encode(line)
    own = lax.all_to_all(
        jnp.broadcast_to(coded[None], (group,) + coded.shape), "param", split_axis=0, concat_axis=0, tiled=True
    )
    other = lax.ppermute(own, "ex", [(i, i ^ 1) for i in range(ex_size)])

    block = (out_tiles * width // group, out_tiles * width // ex_size)
    place = jnp.stack([ex, param]).astype(jnp.int32)
    return factor(place, owner_map, own, other, group * ex_size, out_tiles, block)


def solution(mesh):
    placed = (P("ex", "param"), P("ex", "param"), P(), P(), P(), P(), P(), P(), P("ex", None))
    return jax.shard_map(
        functools.partial(per_device, mesh.shape["ex"]),
        mesh=mesh,
        in_specs=placed,
        out_specs=(P(("ex", "param"), None), P("param", "ex")),
        check_vma=False,
    )
```
